32 devices in a mesh: grp: 2 (over y), own: 8 (over z, x), tile: 2 (over core).
Axes of the slice: x: 2, y: 2, z: 4, core: 2. Of those that a mesh axis runs over, the one named last changes fastest.
Arguments:
- known: bfloat16 [32, 512, 1536], P(('grp', 'own'), None, 'tile'), parts along dimension 0, may hold values from -6 to 6
- outer_blocks: bfloat16 [256, 512, 512], P(('grp', 'own')), parts along dimension 0, may hold values from -0.0625 to 0.0625
- outer_row: int32 [256], P(('grp', 'own')), parts along dimension 0, may hold values from 0 to 15, as said below
- outer_col: int32 [256], P(('grp', 'own')), parts along dimension 0, may hold values from 0 to 7, as said below
- right_side: bfloat16 [16, 512, 1536], P('grp', 'own', 'tile'), parts along dimension 0, may hold values from -6 to 6
- window_blocks: bfloat16 [16, 8, 512, 512], P('grp', None, 'own'), parts along dimension 0, may hold values from -0.125 to 0.125
- window_pattern: int32 [16, 8], P('grp'), parts along dimension 0, may hold values from 0 to 1, as said below
- diag_inverse: bfloat16 [16, 512, 512], P('grp', None, 'own'), parts along dimension 0, may hold values from -1 to 2, as said below
Outputs:
- solution: bfloat16 [16, 512, 1536], P('grp', 'own', 'tile'), parts along dimension 0
The draws below stay inside these ranges and needn't reach their ends.
There are 2 independent parts, one for each index of `grp`. The reference program is written for one: setup_inputs(seed, part) draws one part's arguments, and reference() takes and returns one part's arrays. A program takes and returns all parts, laid end to end along the dimension named above; each array names one. Nothing has to cross between parts.
Inputs may be any that keep to these rules, and one draw needn't show every extreme that they name: `outer_row`: block b lies in one of the rows 2 * (b // 16) to 2 * (b // 16) + 1, and each of these rows holds some such block. `outer_col`: each window column is named by some block among b // 16 = o, for every o. `window_pattern`: entry [j, k] is 0 unless j > k, and 1 where j = k + 1. `diag_inverse`: each block is lower triangular, with diagonal entries between 0.5 and 2.
All inputs are finite; a program needn't handle non-finite values.
Results may differ from the reference program's by a relative error of at most 0.0068.
Values may be sent and summed in bfloat16 or wider, within the bound.
No kernel may reach another device: no remote copies, remote signals or barrier semaphores. Data moves between devices by JAX's collectives and lax.ppermute only.
A program may use at most 128 MiB of HBM per device.

```python
import math
import jax
import jax.numpy as jnp
from jax import lax

SUPER = 512
WINDOW = 8
ROWS_DEV = 2
BLK_DEV = 16
SAMPLES = 1536
BEYOND = 16
BLOCKS = 128


def draw_outer_row(key, part):
    owners = BLOCKS // BLK_DEV
    key_list = jax.random.split(jax.random.fold_in(key, 11), owners)
    orders = jax.vmap(lambda item_key: jax.random.permutation(item_key, BLK_DEV))(key_list)
    local_rows = orders % ROWS_DEV
    global_rows = jnp.arange(owners, dtype=jnp.int32)[:, None] * ROWS_DEV + local_rows
    return global_rows.reshape(-1).astype(jnp.int32)


def draw_outer_col(key, part):
    owners = BLOCKS // BLK_DEV
    first_key, second_key = jax.random.split(jax.random.fold_in(key, 23))
    key_list = jax.random.split(first_key, owners)
    orders = jax.vmap(lambda item_key: jax.random.permutation(item_key, BLK_DEV))(key_list)
    extra = jax.random.randint(second_key, (owners, BLK_DEV), 0, WINDOW)
    columns = jnp.where(orders < WINDOW, orders, extra)
    return columns.reshape(-1).astype(jnp.int32)


def draw_window_pattern(key, part):
    bits = jax.random.randint(jax.random.fold_in(key, 37), (WINDOW, WINDOW), 0, 5) < 3
    row_pos = lax.broadcasted_iota(jnp.int32, (WINDOW, WINDOW), 0)
    col_pos = lax.broadcasted_iota(jnp.int32, (WINDOW, WINDOW), 1)
    below = jnp.where(row_pos > col_pos, bits.astype(jnp.int32), 0)
    return jnp.where(row_pos == col_pos + 1, 1, below).astype(jnp.int32)


def draw_diag_inverse(key, part):
    key_off, key_diag = jax.random.split(jax.random.fold_in(key, 41))
    shape = (WINDOW, SUPER, SUPER)
    row_pos = lax.broadcasted_iota(jnp.int32, shape, 1)
    col_pos = lax.broadcasted_iota(jnp.int32, shape, 2)
    off_part = jax.random.normal(key_off, shape, jnp.float32) * (0.6 / math.sqrt(SUPER))
    diag_part = jax.random.uniform(key_diag, shape, jnp.float32, 0.7, 1.4)
    matrix = jnp.where(row_pos > col_pos, off_part, 0.0) + jnp.where(row_pos == col_pos, diag_part, 0.0)
    return matrix.astype(jnp.bfloat16)


def level_of(own_key, extent, pieces, low, high):
    gain, own = 1.0, jax.random.fold_in(own_key, 6)
    for dim, blocks in pieces:
        draws = jnp.exp(jax.random.uniform(jax.random.fold_in(own, dim), (blocks,), jnp.float32, low / len(pieces), high / len(pieces)))
        gain = gain * jnp.repeat(draws, extent[dim] // blocks).reshape([-1 if axis == dim else 1 for axis in range(len(extent))])
    return gain


def gaussian(own_key, dims, width, most, shards=(), kind=jnp.bfloat16):
    loudness = level_of(own_key, dims, shards, -0.22, 0.18) if shards else 1.0
    entries = jax.random.normal(own_key, dims, jnp.float32) * width * loudness
    return jnp.minimum(jnp.maximum(entries, -most), most).astype(kind)


def setup_inputs(seed: int = 0, part: int = 0) -> dict:
    keys = jax.random.split(jax.random.key(seed), 9)
    own_keys = jax.random.split(jax.random.fold_in(keys[8], part), 9)
    known = gaussian(own_keys[0], (BEYOND, SUPER, SAMPLES), 1.0, 6.0, ((0, 8), (2, 2)))
    outer_blocks = gaussian(own_keys[1], (BLOCKS, SUPER, SUPER), (SUPER * BLOCKS // WINDOW) ** -0.5, 0.0625, ((0, 8),))
    outer_row = draw_outer_row(jax.random.fold_in(jax.random.fold_in(keys[8], part), 71), part)
    outer_col = draw_outer_col(jax.random.fold_in(jax.random.fold_in(keys[8], part), 71), part)
    right_side = gaussian(own_keys[4], (WINDOW, SUPER, SAMPLES), 1.0, 6.0, ((1, 8), (2, 2)))
    window_blocks = gaussian(own_keys[5], (WINDOW, WINDOW, SUPER, SUPER), (SUPER * WINDOW // 2) ** -0.5, 0.125, ((2, 8),))
    window_pattern = draw_window_pattern(jax.random.fold_in(jax.random.fold_in(keys[8], part), 71), part)
    diag_inverse = draw_diag_inverse(jax.random.fold_in(jax.random.fold_in(keys[8], part), 71), part)
    return {"known": known, "outer_blocks": outer_blocks, "outer_row": outer_row, "outer_col": outer_col, "right_side": right_side, "window_blocks": window_blocks, "window_pattern": window_pattern, "diag_inverse": diag_inverse}


def reference(known, outer_blocks, outer_row, outer_col, right_side, window_blocks, window_pattern, diag_inverse):
    def scan_block(totals, item):
        factor_block, source_row, target_col = item
        source = known[source_row.astype(jnp.int32)]
        product = lax.dot_general(factor_block, source, (((0,), (0,)), ((), ())), preferred_element_type=jnp.float32)
        return totals.at[target_col.astype(jnp.int32)].add(product), None

    outer_sum, _ = lax.scan(scan_block, jnp.zeros((WINDOW, SUPER, SAMPLES), jnp.float32), (outer_blocks, outer_row, outer_col))
    solution = jnp.zeros((WINDOW, SUPER, SAMPLES), jnp.bfloat16)
    for column in reversed(range(WINDOW)):
        pattern_mask = window_pattern[:, column].astype(jnp.float32)
        weighted = solution.astype(jnp.float32) * pattern_mask[:, None, None]
        window_term = jnp.einsum("jrc,jrs->cs", window_blocks[:, column].astype(jnp.float32), weighted)
        residual = right_side[column].astype(jnp.float32) - outer_sum[column] - window_term
        rounded = residual.astype(jnp.bfloat16)
        value = lax.dot_general(diag_inverse[column], rounded, (((0,), (0,)), ((), ())), preferred_element_type=jnp.float32)
        solution = solution.at[column].set(value.astype(jnp.bfloat16))
    return solution
```

```python
import functools

import jax
import jax.numpy as jnp
from jax import lax
from jax.experimental import pallas as pl
from jax.experimental.pallas import tpu as pltpu
from jax.sharding import PartitionSpec as P

F32, BF16 = jnp.float32, jnp.bfloat16
VMEM_LIMIT = 50 * 1024 * 1024
STAGES = ((7, 6, 5, 4), (3, 2, 1, 0))
CHUNK = 2

SMEM_SPEC = pl.BlockSpec(memory_space=pltpu.SMEM)
VMEM_SPEC = pl.BlockSpec(memory_space=pltpu.VMEM)
ANY_SPEC = pl.BlockSpec(memory_space=pl.ANY)


def params(**extra):
    return pltpu.CompilerParams(vmem_limit_bytes=VMEM_LIMIT, **extra)


def stage_blocks(columns):
    blocks = []
    for place, k in enumerate(columns):
        blocks += [(j, k) for j in columns[:place]] + [(k, k)]
    return blocks


def weights_kernel(stages, meta, window_ref, diag_ref, *refs):
    outs, (turned, sems) = refs[: len(stages)], refs[len(stages) :]
    half = outs[0].shape[1]
    start = pl.multiple_of(meta[2] * half, half)
    copies = []
    for out, columns in zip(outs, stages):
        for place, (j, k) in enumerate(stage_blocks(columns)):
            if j != k:
                copy = pltpu.make_async_copy(
                    window_ref.at[j, k, pl.ds(start, half)], out.at[place], sems.at[len(copies)]
                )
                copy.start()
                copies.append(copy)
    for out, columns in zip(outs, stages):
        for place, (j, k) in enumerate(stage_blocks(columns)):
            if j == k:
                turned[k] = diag_ref[k].T
                copy = pltpu.make_async_copy(
                    turned.at[k, pl.ds(start, half)], out.at[place], sems.at[len(copies)]
                )
                copy.start()
                copies.append(copy)
    for copy in copies:
        copy.wait()


def gather_weights(meta, window_blocks, diag_inverse, stages):
    columns, super_size, rows = diag_inverse.shape
    shapes = [
        jax.ShapeDtypeStruct((len(stage_blocks(c)), rows // 2, super_size), BF16) for c in stages
    ]
    total = sum(s.shape[0] for s in shapes)
    parts = pl.pallas_call(
        functools.partial(weights_kernel, stages),
        out_shape=shapes,
        in_specs=[SMEM_SPEC, ANY_SPEC, VMEM_SPEC],
        out_specs=[ANY_SPEC] * len(shapes),
        scratch_shapes=[
            pltpu.VMEM((columns, rows, super_size), BF16),
            pltpu.SemaphoreType.DMA((total,)),
        ],
        compiler_params=params(),
        name="own_weights",
    )(meta, window_blocks, diag_inverse)
    return [lax.all_gather(p, ("own", "tile"), axis=0, tiled=False) for p in parts]


def store_split(total, kk, side, send, keep):
    rows = send.shape[1]
    send[kk] = total[pl.ds(pl.multiple_of((1 - side) * rows, rows), rows)].astype(BF16)
    keep[kk] = total[pl.ds(pl.multiple_of(side * rows, rows), rows)]


def outer_kernel(columns, split, meta, row_ref, col_ref, known, draws, blocks, *refs):
    outs, (turned, slab, total, sems) = refs[:-4], refs[-4:]
    high, low = columns[0], columns[-1]
    count, rows_dev = blocks.shape[0], known.shape[0]

    def block_copy(b):
        return pltpu.make_async_copy(blocks.at[b], slab.at[b], sems.at[b])

    def start(b, _):
        @pl.when((col_ref[b] >= low) & (col_ref[b] <= high))
        def _():
            block_copy(b).start()

        return 0

    lax.fori_loop(0, count, start, 0)
    for r in range(rows_dev):
        turned[r] = known[r].T
    rows = draws.shape[1]
    place = lax.broadcasted_iota(jnp.int32, (rows, total.shape[1]), 0) + meta[0] * rows
    lane = lax.broadcasted_iota(jnp.int32, (rows, total.shape[1]), 1)
    spread = jnp.where(place == lane, 1.0, 0.0).astype(BF16)

    def column(kk, _):
        k = high - kk
        total[...] = jnp.dot(draws[k].T, spread, preferred_element_type=F32)

        def block(b, _):
            @pl.when(col_ref[b] == k)
            def _():
                block_copy(b).wait()
                source = row_ref[b] - meta[0] * rows_dev
                total[...] -= jnp.dot(turned[source], slab[b], preferred_element_type=F32)

            return 0

        lax.fori_loop(0, count, block, 0)
        if split:
            store_split(total, kk, meta[1], *outs)
        else:
            outs[0][kk] = total[...]
        return 0

    lax.fori_loop(0, len(columns), column, 0)


def outer_terms(meta, outer_row, outer_col, known, right_side, outer_blocks, columns, split):
    rows_dev, super_size, samples = known.shape
    count, n = outer_blocks.shape[0], len(columns)
    if split:
        shapes = [
            jax.ShapeDtypeStruct((n, samples // 2, super_size), BF16),
            jax.ShapeDtypeStruct((n, samples // 2, super_size), F32),
        ]
    else:
        shapes = [jax.ShapeDtypeStruct((n, samples, super_size), F32)]
    return pl.pallas_call(
        functools.partial(outer_kernel, columns, split),
        out_shape=shapes,
        in_specs=[SMEM_SPEC] * 3 + [VMEM_SPEC, VMEM_SPEC, ANY_SPEC],
        out_specs=[VMEM_SPEC] * len(shapes),
        scratch_shapes=[
            pltpu.VMEM((rows_dev, samples, super_size), BF16),
            pltpu.VMEM((count, super_size, super_size), BF16),
            pltpu.VMEM((samples, super_size), F32),
            pltpu.SemaphoreType.DMA((count,)),
        ],
        compiler_params=params(),
        cost_estimate=pl.CostEstimate(
            flops=4 * n * samples * super_size * super_size,
            bytes_accessed=4 * n * samples * super_size,
            transcendentals=0,
        ),
        name="outer_terms",
    )(meta, outer_row, outer_col, known, right_side, outer_blocks)


def cross_kernel(chunk, before, meta, pattern, base, window, *refs):
    solved, (send, keep, joined, total) = refs[: len(before)], refs[len(before) :]
    piece = solved[0].shape[1]
    lanes = 0
    for ref, columns in zip(solved, before):
        width = ref.shape[2]
        for o in range(ref.shape[0]):
            z, x = o // 2, o % 2
            start = (x * (ref.shape[0] // 2) + z) * piece
            joined[start : start + piece, lanes : lanes + width] = ref[o]
        lanes += width
    earlier = [j for columns in before for j in columns]
    for kk, k in enumerate(chunk):
        block = jnp.concatenate(
            [window[j, k] * pattern[j, k].astype(F32).astype(BF16) for j in earlier], axis=0
        )
        total[...] = base[kk] - jnp.dot(joined[...], block, preferred_element_type=F32)
        store_split(total, kk, meta[1], send, keep)


def cross_terms(meta, pattern, base, window_blocks, solved, chunk, before):
    n, samples, super_size = base.shape
    rows = window_blocks.shape[2]
    return pl.pallas_call(
        functools.partial(cross_kernel, chunk, before),
        out_shape=[
            jax.ShapeDtypeStruct((n, samples // 2, super_size), BF16),
            jax.ShapeDtypeStruct((n, samples // 2, super_size), F32),
        ],
        in_specs=[SMEM_SPEC, SMEM_SPEC] + [VMEM_SPEC] * (2 + len(solved)),
        out_specs=[VMEM_SPEC] * 2,
        scratch_shapes=[
            pltpu.VMEM((samples, rows * sum(len(c) for c in before)), BF16),
            pltpu.VMEM((samples, super_size), F32),
        ],
        compiler_params=params(),
        name="cross_terms",
    )(meta, pattern, base, window_blocks, *solved)


def add_kernel(meta, keep, got, *outs):
    piece = outs[0].shape[1]
    for kk in range(keep.shape[0]):
        for d, out in enumerate(outs):
            rows = pl.ds(pl.multiple_of(meta[4 + d] * piece, piece), piece)
            out[kk] = (keep[kk, rows] + got[kk, rows].astype(F32)).astype(out.dtype)


def scatter_sum(meta, send, keep, owners):
    pair_swap = [(o, o ^ 1) for o in range(owners)]
    got = lax.ppermute(send, "own", pair_swap)
    n, half, super_size = keep.shape
    depth = owners // 2
    shapes = [
        jax.ShapeDtypeStruct((n, half // depth, super_size), F32 if d == 0 else BF16)
        for d in range(depth)
    ]
    parts = pl.pallas_call(
        add_kernel,
        out_shape=shapes,
        in_specs=[SMEM_SPEC, VMEM_SPEC, VMEM_SPEC],
        out_specs=[VMEM_SPEC] * depth,
        compiler_params=params(),
        name="pair_sum",
    )(meta, keep, got)
    moved = [
        lax.ppermute(parts[d], "own", [(o, o ^ (2 * d)) for o in range(owners)])
        for d in range(1, depth)
    ]
    return [parts[0]] + moved


def solve_kernel(columns, pattern, weights, *refs):
    chunks = (len(refs) - 3) // 4
    parts, (out, slab, sems) = refs[: 4 * chunks], refs[4 * chunks :]
    blocks = stage_blocks(columns)
    copies = []
    for place in range(len(blocks)):
        copy = pltpu.make_async_copy(weights.at[:, place], slab.at[place], sems.at[place])
        copy.start()
        copies.append(copy)
    size = slab.shape[3]
    done, place = {}, 0
    per = len(columns) // chunks
    width = size // out.shape[0]
    for index, k in enumerate(columns):
        mine = parts[4 * (index // per) : 4 * (index // per) + 4]
        value = mine[0][index % per]
        for part in mine[1:]:
            value = value + part[index % per].astype(F32)
        for j in columns[:index]:
            copies[place].wait()
            block = slab[place].reshape(size, size)
            value = value - pattern[j, k].astype(F32) * jnp.dot(
                done[j], block, preferred_element_type=F32
            )
            place += 1
        copies[place].wait()
        block = slab[place].reshape(size, size)
        done[k] = lax.dot_general(
            value.astype(BF16), block, (((1,), (1,)), ((), ())), preferred_element_type=F32
        ).astype(BF16)
        place += 1
        for o in range(out.shape[0]):
            out[o, :, index * width : (index + 1) * width] = done[k][:, o * width : (o + 1) * width]


def solve_stage(pattern, weights, chunks, columns, owners):
    pieces, count, rows, super_size = weights.shape
    piece = chunks[0][0].shape[1]
    width = super_size // owners
    flat = [part for parts in chunks for part in parts]
    return pl.pallas_call(
        functools.partial(solve_kernel, columns),
        out_shape=jax.ShapeDtypeStruct((owners, piece, width * len(columns)), BF16),
        in_specs=[SMEM_SPEC, ANY_SPEC] + [VMEM_SPEC] * len(flat),
        out_specs=VMEM_SPEC,
        scratch_shapes=[
            pltpu.VMEM((count, pieces, rows, super_size), BF16),
            pltpu.SemaphoreType.DMA((count,)),
        ],
        compiler_params=params(),
        name="solve_stage",
    )(pattern, weights, *flat)


def place_kernel(stages, *refs):
    solved, (out, joined) = refs[: len(stages)], refs[len(stages) :]
    owners, piece = solved[0].shape[0], solved[0].shape[1]
    rows = out.shape[1]
    for ref, columns in zip(solved, stages):
        for first in range(0, len(columns), 2):
            for o in range(owners):
                joined[o * piece : (o + 1) * piece] = ref[o, :, first * rows : (first + 2) * rows]
            flipped = joined[...].T
            out[columns[first]] = flipped[:rows]
            out[columns[first + 1]] = flipped[rows:]


def place_rows(solved, stages, columns, rows):
    owners, piece, _ = solved[0].shape
    return pl.pallas_call(
        functools.partial(place_kernel, stages),
        out_shape=jax.ShapeDtypeStruct((columns, rows, owners * piece), BF16),
        in_specs=[VMEM_SPEC] * len(solved),
        out_specs=VMEM_SPEC,
        scratch_shapes=[pltpu.VMEM((owners * piece, 2 * rows), BF16)],
        compiler_params=params(),
        name="place_rows",
    )(*solved)


def staged_body(
    owners,
    known,
    outer_blocks,
    outer_row,
    outer_col,
    right_side,
    window_blocks,
    window_pattern,
    diag_inverse,
):
    own = lax.axis_index("own")
    z, x = own // 2, own % 2
    meta = jnp.stack([own, x, lax.axis_index("tile"), z, z, z ^ 1, z ^ 2, z ^ 3]).astype(jnp.int32)
    weights = gather_weights(meta, window_blocks, diag_inverse, STAGES)
    solved = []
    for stage, columns in enumerate(STAGES):
        chunks = []
        for first in range(0, len(columns), CHUNK):
            chunk = columns[first : first + CHUNK]
            outer = outer_terms(
                meta, outer_row, outer_col, known, right_side, outer_blocks, chunk, stage == 0
            )
            if stage == 0:
                send, keep = outer
            else:
                send, keep = cross_terms(
                    meta, window_pattern, outer[0], window_blocks, solved, chunk, STAGES[:stage]
                )
            chunks.append(scatter_sum(meta, send, keep, owners))
        mine = solve_stage(window_pattern, weights[stage], chunks, columns, owners)
        solved.append(lax.all_to_all(mine, "own", 0, 0, tiled=True))
    solved = [
        s.reshape(owners // 2, 2, *s.shape[1:]).swapaxes(0, 1).reshape(s.shape) for s in solved
    ]
    return place_rows(solved, STAGES, right_side.shape[0], right_side.shape[1])


def plain_body(
    known,
    outer_blocks,
    outer_row,
    outer_col,
    right_side,
    window_blocks,
    window_pattern,
    diag_inverse,
):
    owner_index = lax.axis_index("own")
    columns = right_side.shape[0]
    rows_dev = right_side.shape[1]
    super_size = window_blocks.shape[3]
    sample_count = known.shape[2]
    local_row = outer_row - owner_index * known.shape[0]

    def add_block(block_index, totals):
        factor_block = lax.dynamic_index_in_dim(outer_blocks, block_index, 0, keepdims=False)
        source_row = lax.dynamic_index_in_dim(local_row, block_index, 0, keepdims=False)
        target_col = lax.dynamic_index_in_dim(outer_col, block_index, 0, keepdims=False)
        source = lax.dynamic_index_in_dim(known, source_row, 0, keepdims=False)
        product = lax.dot_general(
            factor_block, source, (((0,), (0,)), ((), ())), preferred_element_type=F32
        )
        current = lax.dynamic_index_in_dim(totals, target_col, 0, keepdims=False)
        return lax.dynamic_update_index_in_dim(totals, current + product, target_col, 0)

    outer_sum = lax.fori_loop(
        0,
        outer_blocks.shape[0],
        add_block,
        jnp.zeros((columns, super_size, sample_count), F32),
    )
    solved = jnp.zeros((columns, rows_dev, sample_count), BF16)
    for column in reversed(range(columns)):
        local_term = lax.dynamic_update_slice(
            jnp.zeros((super_size, sample_count), F32),
            right_side[column].astype(F32),
            (owner_index * rows_dev, jnp.zeros((), jnp.int32)),
        )
        pattern_mask = window_pattern[:, column].astype(BF16)
        weighted = solved * pattern_mask[:, None, None]
        window_term = jnp.einsum(
            "jrc,jrs->cs", window_blocks[:, column], weighted, preferred_element_type=F32
        )
        residual = lax.psum(local_term - outer_sum[column] - window_term, "own")
        values = lax.dot_general(
            diag_inverse[column],
            residual.astype(BF16),
            (((0,), (0,)), ((), ())),
            preferred_element_type=F32,
        )
        solved = solved.at[column].set(values.astype(BF16))
    return solved


def solution(mesh):
    owners = mesh.shape["own"]
    body = functools.partial(staged_body, owners) if owners == 8 else plain_body
    return jax.shard_map(
        body,
        mesh=mesh,
        in_specs=(
            P(("grp", "own"), None, "tile"),
            P(("grp", "own"), None, None),
            P(("grp", "own")),
            P(("grp", "own")),
            P("grp", "own", "tile"),
            P("grp", None, "own", None),
            P("grp", None),
            P("grp", None, "own"),
        ),
        out_specs=P("grp", "own", "tile"),
        check_vma=False,
    )
```

```python
import functools

import jax
import jax.numpy as jnp
from jax import lax
from jax.experimental import pallas as pl
from jax.experimental.pallas import tpu as pltpu
from jax.sharding import PartitionSpec as P

F32, BF16 = jnp.float32, jnp.bfloat16
VMEM_LIMIT = 50 * 1024 * 1024
STAGES = ((7, 6, 5, 4), (3, 2, 1, 0))
CHUNKS = (((7, 6), (5, 4)), ((3, 2), (1,), (0,)))

SMEM_SPEC = pl.BlockSpec(memory_space=pltpu.SMEM)
VMEM_SPEC = pl.BlockSpec(memory_space=pltpu.VMEM)
ANY_SPEC = pl.BlockSpec(memory_space=pl.ANY)


def params(**extra):
    return pltpu.CompilerParams(vmem_limit_bytes=VMEM_LIMIT, **extra)


def stage_blocks(columns):
    blocks = []
    for place, k in enumerate(columns):
        blocks += [(j, k) for j in columns[:place]] + [(k, k)]
    return blocks


def weights_kernel(stages, meta, window_ref, diag_ref, *refs):
    outs, (turned, sems) = refs[-2 - len(stages) : -2], refs[-2:]
    half, rows = outs[0].shape[2], window_ref.shape[2]
    start = pl.multiple_of(meta[2] * half, half)
    copies = []

    def move(source, target):
        copy = pltpu.make_async_copy(source, target, sems.at[len(copies)])
        copy.start()
        copies.append(copy)

    blocks = [
        (out.at[0, place], j, k)
        for out, columns in zip(outs, stages)
        for place, (j, k) in enumerate(stage_blocks(columns))
    ]
    for target, j, k in blocks:
        if j != k:
            move(window_ref.at[j, k, pl.ds(start, half)], target)
    lane = lax.broadcasted_iota(jnp.int32, (half, rows), 1)
    pick = jnp.where(lane == lax.broadcasted_iota(jnp.int32, (half, rows), 0) + start, 1.0, 0.0)
    pick = pick.astype(BF16)
    for target, j, k in blocks:
        if j == k:
            turned[k] = lax.dot_general(
                pick, diag_ref[k], (((1,), (1,)), ((), ())), preferred_element_type=F32
            ).astype(BF16)
            move(turned.at[k], target)
    for copy in copies:
        copy.wait()


def own_weights(meta, window_blocks, diag_inverse, columns, after):
    count, super_size, rows = diag_inverse.shape
    blocks = len(stage_blocks(columns))
    return pl.pallas_call(
        functools.partial(weights_kernel, (columns,)),
        out_shape=jax.ShapeDtypeStruct((1, blocks, rows // 2, super_size), BF16),
        in_specs=[SMEM_SPEC, ANY_SPEC, VMEM_SPEC] + [ANY_SPEC] * len(after),
        out_specs=ANY_SPEC,
        scratch_shapes=[
            pltpu.VMEM((count, rows // 2, super_size), BF16),
            pltpu.SemaphoreType.DMA((blocks,)),
        ],
        compiler_params=params(),
        name="own_weights",
    )(meta, window_blocks, diag_inverse, *after)


def join_kernel(left, right, *refs):
    out, sems = refs[-2:]
    half = out.shape[0] // 2
    copies = [
        pltpu.make_async_copy(source, out.at[pl.ds(i * half, half)], sems.at[i])
        for i, source in enumerate((left, right))
    ]
    for copy in copies:
        copy.start()
    for copy in copies:
        copy.wait()


def join(left, right, after):
    return pl.pallas_call(
        join_kernel,
        out_shape=jax.ShapeDtypeStruct((2 * left.shape[0], *left.shape[1:]), left.dtype),
        in_specs=[ANY_SPEC] * (2 + len(after)),
        out_specs=ANY_SPEC,
        scratch_shapes=[pltpu.SemaphoreType.DMA((2,))],
        compiler_params=params(),
        name="join",
    )(left, right, *after)


def hold_kernel(source, *refs):
    out, sem = refs[-2:]
    copy = pltpu.make_async_copy(source, out, sem)
    copy.start()
    copy.wait()


def hold(source, after):
    return pl.pallas_call(
        hold_kernel,
        out_shape=jax.ShapeDtypeStruct(source.shape, source.dtype),
        in_specs=[ANY_SPEC] * (1 + len(after)),
        out_specs=ANY_SPEC,
        scratch_shapes=[pltpu.SemaphoreType.DMA],
        compiler_params=params(),
        name="hold",
    )(source, *after)


def z_move(part, d, owners):
    return lax.ppermute(part, "own", [(o, o ^ (2 * d)) for o in range(owners)])


def x_move(part, owners):
    return lax.ppermute(part, "own", [(o, o ^ 1) for o in range(owners)])


def other_core(parts):
    return [lax.ppermute(w, "tile", [(0, 1), (1, 0)]) for w in parts]


def store_split(total, kk, side, send, keep):
    rows = send.shape[1]
    send[kk] = total[pl.ds(pl.multiple_of((1 - side) * rows, rows), rows)].astype(BF16)
    keep[kk] = total[pl.ds(pl.multiple_of(side * rows, rows), rows)]


def outer_kernel(columns, split, meta, row_ref, col_ref, known, draws, blocks, *refs):
    outs, (turned, slab, total, sems) = refs[-4 - (2 if split else 1) : -4], refs[-4:]
    high, low = columns[0], columns[-1]
    count, rows_dev = blocks.shape[0], known.shape[0]

    def block_copy(b):
        return pltpu.make_async_copy(blocks.at[b], slab.at[b], sems.at[b])

    def start(b, _):
        @pl.when((col_ref[b] >= low) & (col_ref[b] <= high))
        def _():
            block_copy(b).start()

        return 0

    lax.fori_loop(0, count, start, 0)
    for r in range(rows_dev):
        turned[r] = known[r].T
    rows = draws.shape[1]
    place = lax.broadcasted_iota(jnp.int32, (rows, total.shape[1]), 0) + meta[0] * rows
    lane = lax.broadcasted_iota(jnp.int32, (rows, total.shape[1]), 1)
    spread = jnp.where(place == lane, 1.0, 0.0).astype(BF16)

    def column(kk, _):
        k = high - kk
        total[...] = jnp.dot(draws[k].T, spread, preferred_element_type=F32)

        def block(b, _):
            @pl.when(col_ref[b] == k)
            def _():
                block_copy(b).wait()
                source = row_ref[b] - meta[0] * rows_dev
                total[...] -= jnp.dot(turned[source], slab[b], preferred_element_type=F32)

            return 0

        lax.fori_loop(0, count, block, 0)
        if split:
            store_split(total, kk, meta[1], *outs)
        else:
            outs[0][kk] = total[...]
        return 0

    lax.fori_loop(0, len(columns), column, 0)


def outer_terms(
    meta, outer_row, outer_col, known, right_side, outer_blocks, columns, split, after
):
    rows_dev, super_size, samples = known.shape
    count, n = outer_blocks.shape[0], len(columns)
    if split:
        shapes = [
            jax.ShapeDtypeStruct((n, samples // 2, super_size), BF16),
            jax.ShapeDtypeStruct((n, samples // 2, super_size), F32),
        ]
    else:
        shapes = [jax.ShapeDtypeStruct((n, samples, super_size), F32)]
    return pl.pallas_call(
        functools.partial(outer_kernel, columns, split),
        out_shape=shapes,
        in_specs=[SMEM_SPEC] * 3
        + [VMEM_SPEC, VMEM_SPEC, ANY_SPEC]
        + [ANY_SPEC] * len(after),
        out_specs=[VMEM_SPEC] * len(shapes),
        scratch_shapes=[
            pltpu.VMEM((rows_dev, samples, super_size), BF16),
            pltpu.VMEM((count, super_size, super_size), BF16),
            pltpu.VMEM((samples, super_size), F32),
            pltpu.SemaphoreType.DMA((count,)),
        ],
        compiler_params=params(),
        name="outer_terms",
    )(meta, outer_row, outer_col, known, right_side, outer_blocks, *after)


def cross_kernel(chunk, offset, before, meta, pattern, base, window, *refs):
    solved, (send, keep, joined, total, blocks, sems) = refs[: len(before)], refs[-6:]
    piece, depth = solved[0].shape[1], solved[0].shape[0] // 2
    rows = window.shape[2]
    earlier = [j for columns in before for j in columns]
    copies = []
    for kk, k in enumerate(chunk):
        for index, j in enumerate(earlier):
            copy = pltpu.make_async_copy(
                window.at[j, k], blocks.at[kk, pl.ds(index * rows, rows)], sems.at[kk, index]
            )
            copy.start()
            copies.append(copy)
    lanes = 0
    for ref in solved:
        width = ref.shape[2]
        for o in range(2 * depth):
            start = ((o % 2) * depth + o // 2) * piece
            joined[start : start + piece, lanes : lanes + width] = ref[o]
        lanes += width
    for copy in copies:
        copy.wait()
    for kk, k in enumerate(chunk):
        for index, j in enumerate(earlier):
            here = pl.ds(index * rows, rows)
            blocks[kk, here] = blocks[kk, here] * pattern[j, k].astype(F32).astype(BF16)
        total[...] = base[kk] - jnp.dot(joined[...], blocks[kk], preferred_element_type=F32)
        store_split(total, kk, meta[1], send, keep)


def cross_terms(meta, pattern, base, window_blocks, solved, chunk, offset, before, after):
    _, samples, super_size = base.shape
    n = len(chunk)
    rows = window_blocks.shape[2]
    earlier = sum(len(c) for c in before)
    return pl.pallas_call(
        functools.partial(cross_kernel, chunk, offset, before),
        out_shape=[
            jax.ShapeDtypeStruct((n, samples // 2, super_size), BF16),
            jax.ShapeDtypeStruct((n, samples // 2, super_size), F32),
        ],
        grid=(1,),
        in_specs=[
            SMEM_SPEC,
            SMEM_SPEC,
            pl.BlockSpec((n, samples, super_size), lambda i: (offset // n, 0, 0)),
            ANY_SPEC,
        ]
        + [VMEM_SPEC] * len(solved)
        + [ANY_SPEC] * len(after),
        out_specs=[VMEM_SPEC] * 2,
        scratch_shapes=[
            pltpu.VMEM((samples, rows * earlier), BF16),
            pltpu.VMEM((samples, super_size), F32),
            pltpu.VMEM((n, rows * earlier, super_size), BF16),
            pltpu.SemaphoreType.DMA((n, earlier)),
        ],
        compiler_params=params(),
        name="cross_terms",
    )(meta, pattern, base, window_blocks, *solved, *after)


def pair_kernel(meta, keep, got, *refs):
    send, mine = refs[-2:]
    piece = send.shape[2]
    for kk in range(keep.shape[0]):
        for d in range(4):
            rows = pl.ds(pl.multiple_of(meta[4 + d] * piece, piece), piece)
            out = mine if d % 2 == 0 else send
            out[d // 2, kk] = (keep[kk, rows] + got[kk, rows].astype(F32)).astype(out.dtype)


def pair_sum(meta, keep, got, owners, after):
    n, half, super_size = keep.shape
    shape = (2, n, half // (owners // 2), super_size)
    return pl.pallas_call(
        pair_kernel,
        out_shape=[jax.ShapeDtypeStruct(shape, BF16), jax.ShapeDtypeStruct(shape, F32)],
        in_specs=[SMEM_SPEC, VMEM_SPEC, VMEM_SPEC] + [ANY_SPEC] * len(after),
        out_specs=[VMEM_SPEC] * 2,
        compiler_params=params(),
        name="pair_sum",
    )(meta, keep, got, *after)


def line_kernel(mine, got, *refs):
    send, keep = refs[-2:]
    keep[...] = mine[0] + got[0].astype(F32)
    send[...] = (mine[1] + got[1].astype(F32)).astype(BF16)


def line_sum(mine, got, after):
    return pl.pallas_call(
        line_kernel,
        out_shape=[
            jax.ShapeDtypeStruct(mine.shape[1:], BF16),
            jax.ShapeDtypeStruct(mine.shape[1:], F32),
        ],
        in_specs=[VMEM_SPEC] * 2 + [ANY_SPEC] * len(after),
        out_specs=[VMEM_SPEC] * 2,
        compiler_params=params(),
        name="line_sum",
    )(mine, got, *after)


def solve_kernel(columns, ready, groups, whole, first, meta, pattern, *refs):
    weights, refs = refs[:4], refs[4:]
    count = 2 * len(groups)
    parts, solved = refs[:count], refs[count : count + len(ready)]
    out, slab, sems = refs[-3:]
    size = slab.shape[3]
    starts = [0]
    for k in [k for group in groups for k in group]:
        starts.append(starts[-1] + columns.index(k) + 1)
    cuts = [(0, starts[1]), (starts[1], starts[-1])] if len(starts) > 2 else [(0, starts[1])]
    copies = {}
    for cut, (low, high) in enumerate(cuts):
        for which, source in enumerate(weights):
            for e, d in enumerate((0, 2, 1, 3)):
                x = meta[1] if which % 2 == 0 else 1 - meta[1]
                t = meta[2] if which < 2 else 1 - meta[2]
                copy = pltpu.make_async_copy(
                    source.at[e, pl.ds(first + low, high - low)],
                    slab.at[pl.ds(low, high - low), (meta[4 + d] * 2 + x) * 2 + t],
                    sems.at[cut, 4 * which + e],
                )
                copy.start()
                copies.setdefault(low, []).append(copy)
    done = {}
    for ref, group in zip(solved, ready):
        for index, j in enumerate(group):
            done[j] = ref[index]
    place = 0

    def next_block():
        for copy in copies.pop(place, ()):
            copy.wait()
        return slab[place].reshape(size, size)

    for g, group in enumerate(groups):
        for index, k in enumerate(group):
            value = parts[2 * g][index] + parts[2 * g + 1][index].astype(F32)
            for j in list(done):
                value = value - pattern[j, k].astype(F32) * jnp.dot(
                    done[j], next_block(), preferred_element_type=F32
                )
                place += 1
            done[k] = lax.dot_general(
                value.astype(BF16),
                next_block(),
                (((1,), (1,)), ((), ())),
                preferred_element_type=F32,
            ).astype(BF16)
            place += 1
    if not whole:
        for index, k in enumerate([k for group in groups for k in group]):
            out[index] = done[k]
    else:
        width = size // out.shape[0]
        for index, k in enumerate(columns):
            for o in range(out.shape[0]):
                here = done[k][:, o * width : (o + 1) * width]
                out[o, :, index * width : (index + 1) * width] = here


def solve(
    meta, pattern, weights, columns, ready, solved, groups, parts, whole, owners, after=()
):
    _, _, rows, super_size = weights[0].shape
    piece = parts[0][0].shape[1]
    before, n = sum(len(g) for g in ready), sum(len(g) for g in groups)
    first, count = before * (before + 1) // 2, n * before + n * (n + 1) // 2
    if whole:
        shape = (owners, piece, super_size // owners * len(columns))
    else:
        shape = (n, piece, super_size)
    flat = [p for part in parts for p in part]
    return pl.pallas_call(
        functools.partial(solve_kernel, columns, ready, groups, whole, first),
        out_shape=jax.ShapeDtypeStruct(shape, BF16),
        in_specs=[SMEM_SPEC] * 2
        + [ANY_SPEC] * 4
        + [VMEM_SPEC] * (len(flat) + len(solved))
        + [ANY_SPEC] * len(after),
        out_specs=VMEM_SPEC,
        scratch_shapes=[
            pltpu.VMEM((count, 2 * owners, rows, super_size), BF16),
            pltpu.SemaphoreType.DMA((2, 2 * owners)),
        ],
        compiler_params=params(),
        name="solve",
    )(meta, pattern, *weights, *flat, *solved, *after)


def place_kernel(stages, *refs):
    solved, (out, joined) = refs[: len(stages)], refs[len(stages) :]
    owners, piece = solved[0].shape[0], solved[0].shape[1]
    rows = out.shape[1]
    for ref, columns in zip(solved, stages):
        for at in range(0, len(columns), 2):
            first = min(at, len(columns) - 2)
            for o in range(owners):
                start = ((o % 2) * (owners // 2) + o // 2) * piece
                joined[start : start + piece] = ref[o, :, first * rows : (first + 2) * rows]
            flipped = joined[...].T
            out[columns[first]] = flipped[:rows]
            out[columns[first + 1]] = flipped[rows:]


def place_rows(solved, stages, columns, rows):
    owners, piece, _ = solved[0].shape
    return pl.pallas_call(
        functools.partial(place_kernel, stages),
        out_shape=jax.ShapeDtypeStruct((columns, rows, owners * piece), BF16),
        in_specs=[VMEM_SPEC] * len(solved),
        out_specs=VMEM_SPEC,
        scratch_shapes=[pltpu.VMEM((owners * piece, 2 * rows), BF16)],
        compiler_params=params(),
        name="place_rows",
    )(*solved)


def staged_body(
    owners,
    known,
    outer_blocks,
    outer_row,
    outer_col,
    right_side,
    window_blocks,
    window_pattern,
    diag_inverse,
):
    own = lax.axis_index("own")
    z, x = own // 2, own % 2
    meta = jnp.stack([own, x, lax.axis_index("tile"), z, z, z ^ 1, z ^ 2, z ^ 3]).astype(jnp.int32)
    first, last = STAGES
    outer = functools.partial(
        outer_terms, meta, outer_row, outer_col, known, right_side, outer_blocks
    )
    weigh = functools.partial(own_weights, meta, window_blocks, diag_inverse)
    own_0 = weigh(first, ())
    opposite_0 = z_move(own_0, 2, owners)
    send_a, keep_a = outer(CHUNKS[0][0], True, (own_0,))
    got_a = x_move(send_a, owners)
    send_b, keep_b = outer(CHUNKS[0][1], True, (send_a,))
    got_b = x_move(send_b, owners)
    (base,) = outer(last, False, (send_b,))
    near_0 = join(own_0, opposite_0, (base,))
    far_0 = z_move(near_0, 1, owners)
    own_1 = weigh(last, (near_0,))
    opposite_1 = z_move(own_1, 2, owners)
    line_a, mine_a = pair_sum(meta, keep_a, got_a, owners, (own_1,))
    across_a = z_move(line_a, 1, owners)
    line_b, mine_b = pair_sum(meta, keep_b, got_b, owners, (line_a,))
    across_b = z_move(line_b, 1, owners)
    line_0 = join(near_0, far_0, (line_b,))
    beside_0 = x_move(line_0, owners)
    end_a, total_a = line_sum(mine_a, across_a, (line_0,))
    last_a = z_move(end_a, 2, owners)
    end_b, total_b = line_sum(mine_b, across_b, (end_a,))
    last_b = z_move(end_b, 2, owners)
    near_1 = join(own_1, opposite_1, (end_b,))
    far_1 = z_move(near_1, 1, owners)
    line_1 = join(near_1, far_1, (beside_0,))
    beside_1 = x_move(line_1, owners)
    weights = [line_0, beside_0, *other_core([line_0, hold(beside_0, (near_1,))])]
    done = solve(
        meta,
        window_pattern,
        weights,
        first,
        (),
        (),
        CHUNKS[0],
        ((total_a, last_a), (total_b, last_b)),
        True,
        owners,
        (line_1,),
    )
    rows_0 = lax.all_to_all(done, "own", 0, 0, tiled=True)
    moved, at = [], 0
    for chunk in CHUNKS[1]:
        send, keep = cross_terms(
            meta, window_pattern, base, window_blocks, (rows_0,), chunk, at, (first,), ()
        )
        moved.append((keep, x_move(send, owners)))
        at += len(chunk)
    parts, after = [], ()
    for keep, got in moved:
        line, mine = pair_sum(meta, keep, got, owners, after)
        end, total = line_sum(mine, z_move(line, 1, owners), ())
        parts.append((total, z_move(end, 2, owners)))
    weights = [line_1, beside_1, *other_core([line_1, beside_1])]
    solved = []
    for index, chunk in enumerate(CHUNKS[1]):
        out = solve(
            meta,
            window_pattern,
            weights,
            last,
            CHUNKS[1][:index],
            solved,
            (chunk,),
            parts[index : index + 1],
            index == len(CHUNKS[1]) - 1,
            owners,
        )
        solved.append(out)
    rows_1 = lax.all_to_all(solved[-1], "own", 0, 0, tiled=True)
    return place_rows([rows_0, rows_1], STAGES, right_side.shape[0], right_side.shape[1])


def plain_body(
    known,
    outer_blocks,
    outer_row,
    outer_col,
    right_side,
    window_blocks,
    window_pattern,
    diag_inverse,
):
    owner_index = lax.axis_index("own")
    columns = right_side.shape[0]
    rows_dev = right_side.shape[1]
    super_size = window_blocks.shape[3]
    sample_count = known.shape[2]
    local_row = outer_row - owner_index * known.shape[0]

    def add_block(block_index, totals):
        factor_block = lax.dynamic_index_in_dim(outer_blocks, block_index, 0, keepdims=False)
        source_row = lax.dynamic_index_in_dim(local_row, block_index, 0, keepdims=False)
        target_col = lax.dynamic_index_in_dim(outer_col, block_index, 0, keepdims=False)
        source = lax.dynamic_index_in_dim(known, source_row, 0, keepdims=False)
        product = lax.dot_general(
            factor_block, source, (((0,), (0,)), ((), ())), preferred_element_type=F32
        )
        current = lax.dynamic_index_in_dim(totals, target_col, 0, keepdims=False)
        return lax.dynamic_update_index_in_dim(totals, current + product, target_col, 0)

    outer_sum = lax.fori_loop(
        0,
        outer_blocks.shape[0],
        add_block,
        jnp.zeros((columns, super_size, sample_count), F32),
    )
    solved = jnp.zeros((columns, rows_dev, sample_count), BF16)
    for column in reversed(range(columns)):
        local_term = lax.dynamic_update_slice(
            jnp.zeros((super_size, sample_count), F32),
            right_side[column].astype(F32),
            (owner_index * rows_dev, jnp.zeros((), jnp.int32)),
        )
        pattern_mask = window_pattern[:, column].astype(BF16)
        weighted = solved * pattern_mask[:, None, None]
        window_term = jnp.einsum(
            "jrc,jrs->cs", window_blocks[:, column], weighted, preferred_element_type=F32
        )
        residual = lax.psum(local_term - outer_sum[column] - window_term, "own")
        values = lax.dot_general(
            diag_inverse[column],
            residual.astype(BF16),
            (((0,), (0,)), ((), ())),
            preferred_element_type=F32,
        )
        solved = solved.at[column].set(values.astype(BF16))
    return solved


def solution(mesh):
    owners = mesh.shape["own"]
    body = functools.partial(staged_body, owners) if owners == 8 else plain_body
    return jax.shard_map(
        body,
        mesh=mesh,
        in_specs=(
            P(("grp", "own"), None, "tile"),
            P(("grp", "own"), None, None),
            P(("grp", "own")),
            P(("grp", "own")),
            P("grp", "own", "tile"),
            P("grp", None, "own", None),
            P("grp", None),
            P("grp", None, "own"),
        ),
        out_specs=P("grp", "own", "tile"),
        check_vma=False,
    )
```

```python
import functools

import jax
import jax.numpy as jnp
from jax import lax
from jax.experimental import pallas as pl
from jax.experimental.pallas import tpu as pltpu
from jax.sharding import PartitionSpec as P

F32, BF16 = jnp.float32, jnp.bfloat16
VMEM_LIMIT = 50 * 1024 * 1024
STAGES = ((7, 6, 5, 4), (3, 2, 1, 0))
CHUNKS = (((7, 6), (5, 4)), ((3, 2), (1,), (0,)))

SMEM_SPEC = pl.BlockSpec(memory_space=pltpu.SMEM)
VMEM_SPEC = pl.BlockSpec(memory_space=pltpu.VMEM)
ANY_SPEC = pl.BlockSpec(memory_space=pl.ANY)


def params(**extra):
    return pltpu.CompilerParams(vmem_limit_bytes=VMEM_LIMIT, **extra)


def stage_blocks(columns):
    blocks = []
    for place, k in enumerate(columns):
        blocks += [(j, k) for j in columns[:place]] + [(k, k)]
    return blocks


def weights_kernel(stages, meta, window_ref, diag_ref, *refs):
    out, turned, sems = refs[-3:]
    half, rows = out.shape[2], window_ref.shape[2]
    start = pl.multiple_of(meta[2] * half, half)
    copies = []

    def move(source, target):
        copy = pltpu.make_async_copy(source, target, sems.at[len(copies)])
        copy.start()
        copies.append(copy)

    pairs = [pair for columns in stages for pair in stage_blocks(columns)]
    blocks = [(out.at[0, place], j, k) for place, (j, k) in enumerate(pairs)]
    for target, j, k in blocks:
        if j != k:
            move(window_ref.at[j, k, pl.ds(start, half)], target)
    lane = lax.broadcasted_iota(jnp.int32, (half, rows), 1)
    pick = jnp.where(lane == lax.broadcasted_iota(jnp.int32, (half, rows), 0) + start, 1.0, 0.0)
    pick = pick.astype(BF16)
    for target, j, k in blocks:
        if j == k:
            turned[k] = lax.dot_general(
                pick, diag_ref[k], (((1,), (1,)), ((), ())), preferred_element_type=F32
            ).astype(BF16)
            move(turned.at[k], target)
    for copy in copies:
        copy.wait()


def own_weights(meta, window_blocks, diag_inverse, stages, after):
    count, super_size, rows = diag_inverse.shape
    blocks = sum(len(stage_blocks(columns)) for columns in stages)
    return pl.pallas_call(
        functools.partial(weights_kernel, stages),
        out_shape=jax.ShapeDtypeStruct((1, blocks, rows // 2, super_size), BF16),
        in_specs=[SMEM_SPEC, ANY_SPEC, VMEM_SPEC] + [ANY_SPEC] * len(after),
        out_specs=ANY_SPEC,
        scratch_shapes=[
            pltpu.VMEM((count, rows // 2, super_size), BF16),
            pltpu.SemaphoreType.DMA((blocks,)),
        ],
        compiler_params=params(),
        name="own_weights",
    )(meta, window_blocks, diag_inverse, *after)


def join_kernel(first, left, right, *refs):
    out, sems = refs[-2:]
    half, here = out.shape[0] // 2, pl.ds(first, out.shape[1])
    copies = [
        pltpu.make_async_copy(source.at[:, here], out.at[pl.ds(i * half, half)], sems.at[i])
        for i, source in enumerate((left, right))
    ]
    for copy in copies:
        copy.start()
    for copy in copies:
        copy.wait()


def join(left, right, after, first=0, count=None):
    count = left.shape[1] if count is None else count
    shape = (2 * left.shape[0], count, *left.shape[2:])
    return pl.pallas_call(
        functools.partial(join_kernel, first),
        out_shape=jax.ShapeDtypeStruct(shape, left.dtype),
        in_specs=[ANY_SPEC] * (2 + len(after)),
        out_specs=ANY_SPEC,
        scratch_shapes=[pltpu.SemaphoreType.DMA((2,))],
        compiler_params=params(),
        name="join",
    )(left, right, *after)


def hold_kernel(source, *refs):
    out, sem = refs[-2:]
    copy = pltpu.make_async_copy(source, out, sem)
    copy.start()
    copy.wait()


def hold(source, after):
    return pl.pallas_call(
        hold_kernel,
        out_shape=jax.ShapeDtypeStruct(source.shape, source.dtype),
        in_specs=[ANY_SPEC] * (1 + len(after)),
        out_specs=ANY_SPEC,
        scratch_shapes=[pltpu.SemaphoreType.DMA],
        compiler_params=params(),
        name="hold",
    )(source, *after)


def z_move(part, d, owners):
    return lax.ppermute(part, "own", [(o, o ^ (2 * d)) for o in range(owners)])


def x_move(part, owners):
    return lax.ppermute(part, "own", [(o, o ^ 1) for o in range(owners)])


def other_core(parts):
    return [lax.ppermute(w, "tile", [(0, 1), (1, 0)]) for w in parts]


def store_split(total, kk, side, send, keep):
    rows = send.shape[1]
    send[kk] = total[pl.ds(pl.multiple_of((1 - side) * rows, rows), rows)].astype(BF16)
    keep[kk] = total[pl.ds(pl.multiple_of(side * rows, rows), rows)]


def outer_kernel(columns, split, meta, row_ref, col_ref, known, draws, blocks, *refs):
    outs, (turned, slab, total, sems) = refs[-4 - (2 if split else 1) : -4], refs[-4:]
    high, low = columns[0], columns[-1]
    count, rows_dev = blocks.shape[0], known.shape[0]

    def block_copy(b):
        return pltpu.make_async_copy(blocks.at[b], slab.at[b], sems.at[b])

    def start(b, _):
        @pl.when((col_ref[b] >= low) & (col_ref[b] <= high))
        def _():
            block_copy(b).start()

        return 0

    lax.fori_loop(0, count, start, 0)
    for r in range(rows_dev):
        turned[r] = known[r].T
    rows = draws.shape[1]
    place = lax.broadcasted_iota(jnp.int32, (rows, total.shape[1]), 0) + meta[0] * rows
    lane = lax.broadcasted_iota(jnp.int32, (rows, total.shape[1]), 1)
    spread = jnp.where(place == lane, 1.0, 0.0).astype(BF16)

    def column(kk, _):
        k = high - kk
        total[...] = jnp.dot(draws[k].T, spread, preferred_element_type=F32)

        def block(b, _):
            @pl.when(col_ref[b] == k)
            def _():
                block_copy(b).wait()
                source = row_ref[b] - meta[0] * rows_dev
                total[...] -= jnp.dot(turned[source], slab[b], preferred_element_type=F32)

            return 0

        lax.fori_loop(0, count, block, 0)
        if split:
            store_split(total, kk, meta[1], *outs)
        else:
            outs[0][kk] = total[...]
        return 0

    lax.fori_loop(0, len(columns), column, 0)


def outer_terms(
    meta, outer_row, outer_col, known, right_side, outer_blocks, columns, split, after
):
    rows_dev, super_size, samples = known.shape
    count, n = outer_blocks.shape[0], len(columns)
    if split:
        shapes = [
            jax.ShapeDtypeStruct((n, samples // 2, super_size), BF16),
            jax.ShapeDtypeStruct((n, samples // 2, super_size), F32),
        ]
    else:
        shapes = [jax.ShapeDtypeStruct((n, samples, super_size), F32)]
    return pl.pallas_call(
        functools.partial(outer_kernel, columns, split),
        out_shape=shapes,
        in_specs=[SMEM_SPEC] * 3
        + [VMEM_SPEC, VMEM_SPEC, ANY_SPEC]
        + [ANY_SPEC] * len(after),
        out_specs=[VMEM_SPEC] * len(shapes),
        scratch_shapes=[
            pltpu.VMEM((rows_dev, samples, super_size), BF16),
            pltpu.VMEM((count, super_size, super_size), BF16),
            pltpu.VMEM((samples, super_size), F32),
            pltpu.SemaphoreType.DMA((count,)),
        ],
        compiler_params=params(),
        name="outer_terms",
    )(meta, outer_row, outer_col, known, right_side, outer_blocks, *after)


def cross_kernel(chunk, offset, before, meta, pattern, base, window, *refs):
    solved, (send, keep, joined, total, blocks, sems) = refs[: len(before)], refs[-6:]
    piece, depth = solved[0].shape[1], solved[0].shape[0] // 2
    rows = window.shape[2]
    earlier = [j for columns in before for j in columns]
    copies = []
    for kk, k in enumerate(chunk):
        for index, j in enumerate(earlier):
            copy = pltpu.make_async_copy(
                window.at[j, k], blocks.at[kk, pl.ds(index * rows, rows)], sems.at[kk, index]
            )
            copy.start()
            copies.append(copy)
    lanes = 0
    for ref in solved:
        width = ref.shape[2]
        for o in range(2 * depth):
            start = ((o % 2) * depth + o // 2) * piece
            joined[start : start + piece, lanes : lanes + width] = ref[o]
        lanes += width
    for copy in copies:
        copy.wait()
    for kk, k in enumerate(chunk):
        for index, j in enumerate(earlier):
            here = pl.ds(index * rows, rows)
            blocks[kk, here] = blocks[kk, here] * pattern[j, k].astype(F32).astype(BF16)
        total[...] = base[kk] - jnp.dot(joined[...], blocks[kk], preferred_element_type=F32)
        store_split(total, kk, meta[1], send, keep)


def cross_terms(meta, pattern, base, window_blocks, solved, chunk, offset, before, after):
    _, samples, super_size = base.shape
    n = len(chunk)
    rows = window_blocks.shape[2]
    earlier = sum(len(c) for c in before)
    return pl.pallas_call(
        functools.partial(cross_kernel, chunk, offset, before),
        out_shape=[
            jax.ShapeDtypeStruct((n, samples // 2, super_size), BF16),
            jax.ShapeDtypeStruct((n, samples // 2, super_size), F32),
        ],
        grid=(1,),
        in_specs=[
            SMEM_SPEC,
            SMEM_SPEC,
            pl.BlockSpec((n, samples, super_size), lambda i: (offset // n, 0, 0)),
            ANY_SPEC,
        ]
        + [VMEM_SPEC] * len(solved)
        + [ANY_SPEC] * len(after),
        out_specs=[VMEM_SPEC] * 2,
        scratch_shapes=[
            pltpu.VMEM((samples, rows * earlier), BF16),
            pltpu.VMEM((samples, super_size), F32),
            pltpu.VMEM((n, rows * earlier, super_size), BF16),
            pltpu.SemaphoreType.DMA((n, earlier)),
        ],
        compiler_params=params(),
        name="cross_terms",
    )(meta, pattern, base, window_blocks, *solved, *after)


def pair_kernel(meta, keep, got, *refs):
    send, mine = refs[-2:]
    piece = send.shape[2]
    for kk in range(keep.shape[0]):
        for d in range(4):
            rows = pl.ds(pl.multiple_of(meta[4 + d] * piece, piece), piece)
            out = mine if d % 2 == 0 else send
            out[d // 2, kk] = (keep[kk, rows] + got[kk, rows].astype(F32)).astype(out.dtype)


def pair_sum(meta, keep, got, owners, after):
    n, half, super_size = keep.shape
    shape = (2, n, half // (owners // 2), super_size)
    return pl.pallas_call(
        pair_kernel,
        out_shape=[jax.ShapeDtypeStruct(shape, BF16), jax.ShapeDtypeStruct(shape, F32)],
        in_specs=[SMEM_SPEC, VMEM_SPEC, VMEM_SPEC] + [ANY_SPEC] * len(after),
        out_specs=[VMEM_SPEC] * 2,
        compiler_params=params(),
        name="pair_sum",
    )(meta, keep, got, *after)


def line_kernel(mine, got, *refs):
    send, keep = refs[-2:]
    keep[...] = mine[0] + got[0].astype(F32)
    send[...] = (mine[1] + got[1].astype(F32)).astype(BF16)


def line_sum(mine, got, after):
    return pl.pallas_call(
        line_kernel,
        out_shape=[
            jax.ShapeDtypeStruct(mine.shape[1:], BF16),
            jax.ShapeDtypeStruct(mine.shape[1:], F32),
        ],
        in_specs=[VMEM_SPEC] * 2 + [ANY_SPEC] * len(after),
        out_specs=[VMEM_SPEC] * 2,
        compiler_params=params(),
        name="line_sum",
    )(mine, got, *after)


def solve_kernel(columns, ready, groups, whole, first, origins, meta, pattern, *refs):
    weights, refs = refs[: len(origins)], refs[len(origins) :]
    count = 2 * len(groups)
    parts, solved = refs[:count], refs[count : count + len(ready)]
    out, slab, sems = refs[-3:]
    size = slab.shape[3]
    starts = [0]
    for k in [k for group in groups for k in group]:
        starts.append(starts[-1] + columns.index(k) + 1)
    cuts = [(0, starts[1]), (starts[1], starts[-1])] if len(starts) > 2 else [(0, starts[1])]
    copies = {}
    for cut, (low, high) in enumerate(cuts):
        for which, (source, (flip_x, flip_core, distances)) in enumerate(zip(weights, origins)):
            for e, d in enumerate(distances):
                x = 1 - meta[1] if flip_x else meta[1]
                t = 1 - meta[2] if flip_core else meta[2]
                copy = pltpu.make_async_copy(
                    source.at[e, pl.ds(first + low, high - low)],
                    slab.at[pl.ds(low, high - low), (meta[4 + d] * 2 + x) * 2 + t],
                    sems.at[cut, len(distances) * which + e],
                )
                copy.start()
                copies.setdefault(low, []).append(copy)
    done = {}
    for ref, group in zip(solved, ready):
        for index, j in enumerate(group):
            done[j] = ref[index]
    place = 0

    def next_block():
        for copy in copies.pop(place, ()):
            copy.wait()
        return slab[place].reshape(size, size)

    for g, group in enumerate(groups):
        for index, k in enumerate(group):
            value = parts[2 * g][index] + parts[2 * g + 1][index].astype(F32)
            for j in list(done):
                value = value - pattern[j, k].astype(F32) * jnp.dot(
                    done[j], next_block(), preferred_element_type=F32
                )
                place += 1
            done[k] = lax.dot_general(
                value.astype(BF16),
                next_block(),
                (((1,), (1,)), ((), ())),
                preferred_element_type=F32,
            ).astype(BF16)
            place += 1
    if not whole:
        for index, k in enumerate([k for group in groups for k in group]):
            out[index] = done[k]
    else:
        width = size // out.shape[0]
        for index, k in enumerate(columns):
            for o in range(out.shape[0]):
                here = done[k][:, o * width : (o + 1) * width]
                out[o, :, index * width : (index + 1) * width] = here


def solve(
    meta, pattern, weights, columns, ready, solved, groups, parts, whole, owners, after=()
):
    arrays, origins = zip(*weights)
    _, _, rows, super_size = arrays[0].shape
    piece = parts[0][0].shape[1]
    before, n = sum(len(g) for g in ready), sum(len(g) for g in groups)
    first, count = before * (before + 1) // 2, n * before + n * (n + 1) // 2
    if whole:
        shape = (owners, piece, super_size // owners * len(columns))
    else:
        shape = (n, piece, super_size)
    flat = [p for part in parts for p in part]
    return pl.pallas_call(
        functools.partial(solve_kernel, columns, ready, groups, whole, first, origins),
        out_shape=jax.ShapeDtypeStruct(shape, BF16),
        in_specs=[SMEM_SPEC] * 2
        + [ANY_SPEC] * len(arrays)
        + [VMEM_SPEC] * (len(flat) + len(solved))
        + [ANY_SPEC] * len(after),
        out_specs=VMEM_SPEC,
        scratch_shapes=[
            pltpu.VMEM((count, 2 * owners, rows, super_size), BF16),
            pltpu.SemaphoreType.DMA((2, 2 * owners)),
        ],
        compiler_params=params(),
        name="solve",
    )(meta, pattern, *arrays, *flat, *solved, *after)


def place_kernel(stages, *refs):
    solved, (out, joined) = refs[: len(stages)], refs[len(stages) :]
    owners, piece = solved[0].shape[0], solved[0].shape[1]
    rows = out.shape[1]
    for ref, columns in zip(solved, stages):
        for at in range(0, len(columns), 2):
            first = min(at, len(columns) - 2)
            for o in range(owners):
                start = ((o % 2) * (owners // 2) + o // 2) * piece
                joined[start : start + piece] = ref[o, :, first * rows : (first + 2) * rows]
            flipped = joined[...].T
            out[columns[first]] = flipped[:rows]
            out[columns[first + 1]] = flipped[rows:]


def place_rows(solved, stages, columns, rows):
    owners, piece, _ = solved[0].shape
    return pl.pallas_call(
        functools.partial(place_kernel, stages),
        out_shape=jax.ShapeDtypeStruct((columns, rows, owners * piece), BF16),
        in_specs=[VMEM_SPEC] * len(solved),
        out_specs=VMEM_SPEC,
        scratch_shapes=[pltpu.VMEM((owners * piece, 2 * rows), BF16)],
        compiler_params=params(),
        name="place_rows",
    )(*solved)


def staged_body(
    owners,
    known,
    outer_blocks,
    outer_row,
    outer_col,
    right_side,
    window_blocks,
    window_pattern,
    diag_inverse,
):
    own = lax.axis_index("own")
    z, x = own // 2, own % 2
    meta = jnp.stack([own, x, lax.axis_index("tile"), z, z, z ^ 1, z ^ 2, z ^ 3]).astype(jnp.int32)
    first, last = STAGES
    outer = functools.partial(
        outer_terms, meta, outer_row, outer_col, known, right_side, outer_blocks
    )
    count_0, count_1 = len(stage_blocks(first)), len(stage_blocks(last))
    own_rows = own_weights(meta, window_blocks, diag_inverse, STAGES, ())
    opposite = z_move(own_rows, 2, owners)
    send_a, keep_a = outer(CHUNKS[0][0], True, (own_rows,))
    got_a = x_move(send_a, owners)
    send_b, keep_b = outer(CHUNKS[0][1], True, (send_a,))
    got_b = x_move(send_b, owners)
    (base,) = outer(last, False, (send_b,))
    near_0 = join(own_rows, opposite, (base,), 0, count_0)
    far_0 = z_move(near_0, 1, owners)
    line_a, mine_a = pair_sum(meta, keep_a, got_a, owners, (near_0,))
    across_a = z_move(line_a, 1, owners)
    line_b, mine_b = pair_sum(meta, keep_b, got_b, owners, (line_a,))
    across_b = z_move(line_b, 1, owners)
    line_0 = join(near_0, far_0, (line_b,))
    beside_0 = x_move(line_0, owners)
    end_a, total_a = line_sum(mine_a, across_a, (line_0,))
    last_a = z_move(end_a, 2, owners)
    end_b, total_b = line_sum(mine_b, across_b, (end_a,))
    last_b = z_move(end_b, 2, owners)
    near_1 = join(own_rows, opposite, (last_b,), count_0, count_1)
    far_1 = z_move(near_1, 1, owners)
    x_near_1 = x_move(near_1, owners)
    core_line, core_beside = other_core([line_0, hold(beside_0, (end_b, last_a))])
    line = (0, 2, 1, 3)
    weights = [
        (line_0, (False, False, line)),
        (beside_0, (True, False, line)),
        (core_line, (False, True, line)),
        (core_beside, (True, True, line)),
    ]
    done = solve(
        meta,
        window_pattern,
        weights,
        first,
        (),
        (),
        CHUNKS[0],
        ((total_a, last_a), (total_b, last_b)),
        True,
        owners,
        (near_1,),
    )
    x_far_1 = x_move(hold(far_1, (x_near_1,)), owners)
    rows_0 = lax.all_to_all(done, "own", 0, 0, tiled=True)
    moved, at = [], 0
    for chunk in CHUNKS[1]:
        send, keep = cross_terms(
            meta, window_pattern, base, window_blocks, (rows_0,), chunk, at, (first,), (x_far_1,) if at else (x_near_1,)
        )
        moved.append((keep, x_move(send, owners)))
        at += len(chunk)
    parts, ends = [], []
    for index, (keep, got) in enumerate(moved):
        part, kept = pair_sum(meta, keep, got, owners, ends[: max(index - 1, 0)])
        before = [moved_end for _, moved_end in parts[: max(index - 1, 0)]]
        end, total = line_sum(kept, z_move(part, 1, owners), before)
        ends.append(end)
        parts.append((total, z_move(end, 2, owners)))
    mine = [join(near_1, far_1, moved[0][:1]), join(x_near_1, x_far_1, moved[-1][:1])]
    weights = [
        (array, (i % 2 > 0, i > 1, line)) for i, array in enumerate(mine + other_core(mine))
    ]
    solve_last = functools.partial(solve, meta, window_pattern, weights, last)
    half = solve_last((), (), CHUNKS[1][:1], parts[:1], False, owners)
    done = solve_last(CHUNKS[1][:1], (half,), CHUNKS[1][1:], parts[1:], True, owners)
    rows_1 = lax.all_to_all(done, "own", 0, 0, tiled=True)
    return place_rows([rows_0, rows_1], STAGES, right_side.shape[0], right_side.shape[1])


def plain_body(
    known,
    outer_blocks,
    outer_row,
    outer_col,
    right_side,
    window_blocks,
    window_pattern,
    diag_inverse,
):
    owner_index = lax.axis_index("own")
    columns = right_side.shape[0]
    rows_dev = right_side.shape[1]
    super_size = window_blocks.shape[3]
    sample_count = known.shape[2]
    local_row = outer_row - owner_index * known.shape[0]

    def add_block(block_index, totals):
        factor_block = lax.dynamic_index_in_dim(outer_blocks, block_index, 0, keepdims=False)
        source_row = lax.dynamic_index_in_dim(local_row, block_index, 0, keepdims=False)
        target_col = lax.dynamic_index_in_dim(outer_col, block_index, 0, keepdims=False)
        source = lax.dynamic_index_in_dim(known, source_row, 0, keepdims=False)
        product = lax.dot_general(
            factor_block, source, (((0,), (0,)), ((), ())), preferred_element_type=F32
        )
        current = lax.dynamic_index_in_dim(totals, target_col, 0, keepdims=False)
        return lax.dynamic_update_index_in_dim(totals, current + product, target_col, 0)

    outer_sum = lax.fori_loop(
        0,
        outer_blocks.shape[0],
        add_block,
        jnp.zeros((columns, super_size, sample_count), F32),
    )
    solved = jnp.zeros((columns, rows_dev, sample_count), BF16)
    for column in reversed(range(columns)):
        local_term = lax.dynamic_update_slice(
            jnp.zeros((super_size, sample_count), F32),
            right_side[column].astype(F32),
            (owner_index * rows_dev, jnp.zeros((), jnp.int32)),
        )
        pattern_mask = window_pattern[:, column].astype(BF16)
        weighted = solved * pattern_mask[:, None, None]
        window_term = jnp.einsum(
            "jrc,jrs->cs", window_blocks[:, column], weighted, preferred_element_type=F32
        )
        residual = lax.psum(local_term - outer_sum[column] - window_term, "own")
        values = lax.dot_general(
            diag_inverse[column],
            residual.astype(BF16),
            (((0,), (0,)), ((), ())),
            preferred_element_type=F32,
        )
        solved = solved.at[column].set(values.astype(BF16))
    return solved


def solution(mesh):
    owners = mesh.shape["own"]
    body = functools.partial(staged_body, owners) if owners == 8 else plain_body
    return jax.shard_map(
        body,
        mesh=mesh,
        in_specs=(
            P(("grp", "own"), None, "tile"),
            P(("grp", "own"), None, None),
            P(("grp", "own")),
            P(("grp", "own")),
            P("grp", "own", "tile"),
            P("grp", None, "own", None),
            P("grp", None),
            P("grp", None, "own"),
        ),
        out_specs=P("grp", "own", "tile"),
        check_vma=False,
    )
```

```python
import functools

import jax
import jax.numpy as jnp
from jax import lax
from jax.experimental import pallas as pl
from jax.experimental.pallas import tpu as pltpu
from jax.sharding import PartitionSpec as P

F32, BF16 = jnp.float32, jnp.bfloat16
VMEM_LIMIT = 50 * 1024 * 1024
STAGES = ((7, 6, 5, 4), (3, 2, 1, 0))
CHUNKS = (((7, 6, 5), (4,)), ((3, 2), (1,), (0,)))

SMEM_SPEC = pl.BlockSpec(memory_space=pltpu.SMEM)
VMEM_SPEC = pl.BlockSpec(memory_space=pltpu.VMEM)
ANY_SPEC = pl.BlockSpec(memory_space=pl.ANY)


def params(**extra):
    return pltpu.CompilerParams(vmem_limit_bytes=VMEM_LIMIT, **extra)


def stage_blocks(columns):
    blocks = []
    for place, k in enumerate(columns):
        blocks += [(j, k) for j in columns[:place]] + [(k, k)]
    return blocks


def weights_kernel(stages, meta, window_ref, diag_ref, *refs):
    out, diag, turned, sems = refs[-4:]
    half, rows = out.shape[2], window_ref.shape[2]
    start = pl.multiple_of(meta[2] * half, half)
    copies = []

    def move(source, target):
        copy = pltpu.make_async_copy(source, target, sems.at[len(copies)])
        copy.start()
        copies.append(copy)

    pairs = [pair for columns in stages for pair in stage_blocks(columns)]
    blocks = [(out.at[0, place], j, k) for place, (j, k) in enumerate(pairs)]
    for target, j, k in blocks:
        if j != k:
            move(window_ref.at[j, k, pl.ds(start, half)], target)
    load = pltpu.make_async_copy(diag_ref, diag, sems.at[len(blocks)])
    load.start()
    lane = lax.broadcasted_iota(jnp.int32, (half, rows), 1)
    pick = jnp.where(lane == lax.broadcasted_iota(jnp.int32, (half, rows), 0) + start, 1.0, 0.0)
    pick = pick.astype(BF16)
    load.wait()
    for target, j, k in blocks:
        if j == k:
            turned[k] = lax.dot_general(
                pick, diag[k], (((1,), (1,)), ((), ())), preferred_element_type=F32
            ).astype(BF16)
            move(turned.at[k], target)
    for copy in copies:
        copy.wait()


def own_weights(meta, window_blocks, diag_inverse, stages, after):
    count, super_size, rows = diag_inverse.shape
    blocks = sum(len(stage_blocks(columns)) for columns in stages)
    return pl.pallas_call(
        functools.partial(weights_kernel, stages),
        out_shape=jax.ShapeDtypeStruct((1, blocks, rows // 2, super_size), BF16),
        in_specs=[SMEM_SPEC, ANY_SPEC, ANY_SPEC] + [ANY_SPEC] * len(after),
        out_specs=ANY_SPEC,
        scratch_shapes=[
            pltpu.VMEM(diag_inverse.shape, BF16),
            pltpu.VMEM((count, rows // 2, super_size), BF16),
            pltpu.SemaphoreType.DMA((blocks + 1,)),
        ],
        compiler_params=params(),
        name="own_weights",
    )(meta, window_blocks, diag_inverse, *after)


def join_kernel(first, left, right, *refs):
    out, sems = refs[-2:]
    half, here = out.shape[0] // 2, pl.ds(first, out.shape[1])
    copies = [
        pltpu.make_async_copy(source.at[:, here], out.at[pl.ds(i * half, half)], sems.at[i])
        for i, source in enumerate((left, right))
    ]
    for copy in copies:
        copy.start()
    for copy in copies:
        copy.wait()


def join(left, right, after, first=0, count=None):
    count = left.shape[1] if count is None else count
    shape = (2 * left.shape[0], count, *left.shape[2:])
    return pl.pallas_call(
        functools.partial(join_kernel, first),
        out_shape=jax.ShapeDtypeStruct(shape, left.dtype),
        in_specs=[ANY_SPEC] * (2 + len(after)),
        out_specs=ANY_SPEC,
        scratch_shapes=[pltpu.SemaphoreType.DMA((2,))],
        compiler_params=params(),
        name="join",
    )(left, right, *after)


def hold_kernel(source, *refs):
    out, sem = refs[-2:]
    copy = pltpu.make_async_copy(source, out, sem)
    copy.start()
    copy.wait()


def hold(source, after):
    return pl.pallas_call(
        hold_kernel,
        out_shape=jax.ShapeDtypeStruct(source.shape, source.dtype),
        in_specs=[ANY_SPEC] * (1 + len(after)),
        out_specs=ANY_SPEC,
        scratch_shapes=[pltpu.SemaphoreType.DMA],
        compiler_params=params(),
        name="hold",
    )(source, *after)


def z_move(part, d, owners):
    return lax.ppermute(part, "own", [(o, o ^ (2 * d)) for o in range(owners)])


def x_move(part, owners):
    return lax.ppermute(part, "own", [(o, o ^ 1) for o in range(owners)])


def other_core(parts):
    return [lax.ppermute(w, "tile", [(0, 1), (1, 0)]) for w in parts]


def store_split(total, kk, side, send, keep):
    rows = send.shape[1]
    send[kk] = total[pl.ds(pl.multiple_of((1 - side) * rows, rows), rows)].astype(BF16)
    keep[kk] = total[pl.ds(pl.multiple_of(side * rows, rows), rows)]


def outer_kernel(columns, split, meta, row_ref, col_ref, known, draws, blocks, *refs):
    outs, (turned, slab, total, sems) = refs[-4 - (2 if split else 1) : -4], refs[-4:]
    high, low = columns[0], columns[-1]
    count, rows_dev = blocks.shape[0], known.shape[0]

    def block_copy(b):
        return pltpu.make_async_copy(blocks.at[b], slab.at[b], sems.at[b])

    def start(b, _):
        @pl.when((col_ref[b] >= low) & (col_ref[b] <= high))
        def _():
            block_copy(b).start()

        return 0

    lax.fori_loop(0, count, start, 0)
    for r in range(rows_dev):
        turned[r] = known[r].T
    rows = draws.shape[1]
    place = lax.broadcasted_iota(jnp.int32, (rows, total.shape[1]), 0) + meta[0] * rows
    lane = lax.broadcasted_iota(jnp.int32, (rows, total.shape[1]), 1)
    spread = jnp.where(place == lane, 1.0, 0.0).astype(BF16)

    def column(kk, _):
        k = high - kk
        total[...] = jnp.dot(draws[k].T, spread, preferred_element_type=F32)

        def block(b, _):
            @pl.when(col_ref[b] == k)
            def _():
                block_copy(b).wait()
                source = row_ref[b] - meta[0] * rows_dev
                total[...] -= jnp.dot(turned[source], slab[b], preferred_element_type=F32)

            return 0

        lax.fori_loop(0, count, block, 0)
        if split:
            store_split(total, kk, meta[1], *outs)
        else:
            outs[0][kk] = total[...]
        return 0

    lax.fori_loop(0, len(columns), column, 0)


def outer_terms(
    meta, outer_row, outer_col, known, right_side, outer_blocks, columns, split, after
):
    rows_dev, super_size, samples = known.shape
    count, n = outer_blocks.shape[0], len(columns)
    if split:
        shapes = [
            jax.ShapeDtypeStruct((n, samples // 2, super_size), BF16),
            jax.ShapeDtypeStruct((n, samples // 2, super_size), F32),
        ]
    else:
        shapes = [jax.ShapeDtypeStruct((n, samples, super_size), F32)]
    return pl.pallas_call(
        functools.partial(outer_kernel, columns, split),
        out_shape=shapes,
        in_specs=[SMEM_SPEC] * 3
        + [VMEM_SPEC, VMEM_SPEC, ANY_SPEC]
        + [ANY_SPEC] * len(after),
        out_specs=[VMEM_SPEC] * len(shapes),
        scratch_shapes=[
            pltpu.VMEM((rows_dev, samples, super_size), BF16),
            pltpu.VMEM((count, super_size, super_size), BF16),
            pltpu.VMEM((samples, super_size), F32),
            pltpu.SemaphoreType.DMA((count,)),
        ],
        compiler_params=params(),
        name="outer_terms",
    )(meta, outer_row, outer_col, known, right_side, outer_blocks, *after)


def cross_kernel(chunk, offset, before, meta, pattern, base, window, *refs):
    solved, (send, keep, joined, total, blocks, sems) = refs[: len(before)], refs[-6:]
    piece, depth = solved[0].shape[1], solved[0].shape[0] // 2
    rows = window.shape[2]
    earlier = [j for columns in before for j in columns]
    copies = []
    for kk, k in enumerate(chunk):
        for index, j in enumerate(earlier):
            copy = pltpu.make_async_copy(
                window.at[j, k], blocks.at[kk, pl.ds(index * rows, rows)], sems.at[kk, index]
            )
            copy.start()
            copies.append(copy)
    lanes = 0
    for ref in solved:
        width = ref.shape[2]
        for o in range(2 * depth):
            start = ((o % 2) * depth + o // 2) * piece
            joined[start : start + piece, lanes : lanes + width] = ref[o]
        lanes += width
    for copy in copies:
        copy.wait()
    for kk, k in enumerate(chunk):
        for index, j in enumerate(earlier):
            here = pl.ds(index * rows, rows)
            blocks[kk, here] = blocks[kk, here] * pattern[j, k].astype(F32).astype(BF16)
        total[...] = base[kk] - jnp.dot(joined[...], blocks[kk], preferred_element_type=F32)
        store_split(total, kk, meta[1], send, keep)


def cross_terms(meta, pattern, base, window_blocks, solved, chunk, offset, before, after):
    _, samples, super_size = base.shape
    n = len(chunk)
    rows = window_blocks.shape[2]
    earlier = sum(len(c) for c in before)
    return pl.pallas_call(
        functools.partial(cross_kernel, chunk, offset, before),
        out_shape=[
            jax.ShapeDtypeStruct((n, samples // 2, super_size), BF16),
            jax.ShapeDtypeStruct((n, samples // 2, super_size), F32),
        ],
        grid=(1,),
        in_specs=[
            SMEM_SPEC,
            SMEM_SPEC,
            pl.BlockSpec((n, samples, super_size), lambda i: (offset // n, 0, 0)),
            ANY_SPEC,
        ]
        + [VMEM_SPEC] * len(solved)
        + [ANY_SPEC] * len(after),
        out_specs=[VMEM_SPEC] * 2,
        scratch_shapes=[
            pltpu.VMEM((samples, rows * earlier), BF16),
            pltpu.VMEM((samples, super_size), F32),
            pltpu.VMEM((n, rows * earlier, super_size), BF16),
            pltpu.SemaphoreType.DMA((n, earlier)),
        ],
        compiler_params=params(),
        name="cross_terms",
    )(meta, pattern, base, window_blocks, *solved, *after)


def pair_kernel(meta, keep, got, *refs):
    send, mine = refs[-2:]
    piece = send.shape[2]
    for kk in range(keep.shape[0]):
        for d in range(4):
            rows = pl.ds(pl.multiple_of(meta[4 + d] * piece, piece), piece)
            out = mine if d % 2 == 0 else send
            out[d // 2, kk] = (keep[kk, rows] + got[kk, rows].astype(F32)).astype(out.dtype)


def pair_sum(meta, keep, got, owners, after):
    n, half, super_size = keep.shape
    shape = (2, n, half // (owners // 2), super_size)
    return pl.pallas_call(
        pair_kernel,
        out_shape=[jax.ShapeDtypeStruct(shape, BF16), jax.ShapeDtypeStruct(shape, F32)],
        in_specs=[SMEM_SPEC, VMEM_SPEC, VMEM_SPEC] + [ANY_SPEC] * len(after),
        out_specs=[VMEM_SPEC] * 2,
        compiler_params=params(),
        name="pair_sum",
    )(meta, keep, got, *after)


def line_kernel(mine, got, *refs):
    send, keep = refs[-2:]
    keep[...] = mine[0] + got[0].astype(F32)
    send[...] = (mine[1] + got[1].astype(F32)).astype(BF16)


def line_sum(mine, got, after):
    return pl.pallas_call(
        line_kernel,
        out_shape=[
            jax.ShapeDtypeStruct(mine.shape[1:], BF16),
            jax.ShapeDtypeStruct(mine.shape[1:], F32),
        ],
        in_specs=[VMEM_SPEC] * 2 + [ANY_SPEC] * len(after),
        out_specs=[VMEM_SPEC] * 2,
        compiler_params=params(),
        name="line_sum",
    )(mine, got, *after)


def solve_kernel(columns, ready, groups, whole, first, origins, meta, pattern, *refs):
    weights, refs = refs[: len(origins)], refs[len(origins) :]
    count = 2 * len(groups)
    sources, solved = refs[:count], refs[count : count + len(ready)]
    parts = refs[-count - 1 : -1]
    out, slab, sems = refs[-count - 4], refs[-count - 3], refs[-count - 2]
    loads = [
        pltpu.make_async_copy(source, part, refs[-1].at[i])
        for i, (source, part) in enumerate(zip(sources, parts))
    ]
    for load in loads:
        load.start()
    size = slab.shape[3]
    starts = [0]
    for k in [k for group in groups for k in group]:
        starts.append(starts[-1] + columns.index(k) + 1)
    cuts = [(0, starts[1]), (starts[1], starts[-1])] if len(starts) > 2 else [(0, starts[1])]
    copies = {}
    for cut, (low, high) in enumerate(cuts):
        for which, (source, (flip_x, flip_core, distances)) in enumerate(zip(weights, origins)):
            for e, d in enumerate(distances):
                x = 1 - meta[1] if flip_x else meta[1]
                t = 1 - meta[2] if flip_core else meta[2]
                copy = pltpu.make_async_copy(
                    source.at[e, pl.ds(first + low, high - low)],
                    slab.at[pl.ds(low, high - low), (meta[4 + d] * 2 + x) * 2 + t],
                    sems.at[cut, len(distances) * which + e],
                )
                copy.start()
                copies.setdefault(low, []).append(copy)
    done = {}
    for ref, group in zip(solved, ready):
        for index, j in enumerate(group):
            done[j] = ref[index]
    place = 0
    for load in loads:
        load.wait()

    def next_block():
        for copy in copies.pop(place, ()):
            copy.wait()
        return slab[place].reshape(size, size)

    for g, group in enumerate(groups):
        for index, k in enumerate(group):
            value = parts[2 * g][index] + parts[2 * g + 1][index].astype(F32)
            for j in list(done):
                value = value - pattern[j, k].astype(F32) * jnp.dot(
                    done[j], next_block(), preferred_element_type=F32
                )
                place += 1
            done[k] = lax.dot_general(
                value.astype(BF16),
                next_block(),
                (((1,), (1,)), ((), ())),
                preferred_element_type=F32,
            ).astype(BF16)
            place += 1
    if not whole:
        for index, k in enumerate([k for group in groups for k in group]):
            out[index] = done[k]
    else:
        width = size // out.shape[0]
        for index, k in enumerate(columns):
            for o in range(out.shape[0]):
                here = done[k][:, o * width : (o + 1) * width]
                out[o, :, index * width : (index + 1) * width] = here


def solve(
    meta, pattern, weights, columns, ready, solved, groups, parts, whole, owners, after=()
):
    arrays, origins = zip(*weights)
    _, _, rows, super_size = arrays[0].shape
    piece = parts[0][0].shape[1]
    before, n = sum(len(g) for g in ready), sum(len(g) for g in groups)
    first, count = before * (before + 1) // 2, n * before + n * (n + 1) // 2
    if whole:
        shape = (owners, piece, super_size // owners * len(columns))
    else:
        shape = (n, piece, super_size)
    flat = [p for part in parts for p in part]
    return pl.pallas_call(
        functools.partial(solve_kernel, columns, ready, groups, whole, first, origins),
        out_shape=jax.ShapeDtypeStruct(shape, BF16),
        in_specs=[SMEM_SPEC] * 2
        + [ANY_SPEC] * len(arrays)
        + [ANY_SPEC] * len(flat)
        + [VMEM_SPEC] * len(solved)
        + [ANY_SPEC] * len(after),
        out_specs=VMEM_SPEC,
        scratch_shapes=[
            pltpu.VMEM((count, 2 * owners, rows, super_size), BF16),
            pltpu.SemaphoreType.DMA((2, 2 * owners)),
            *[pltpu.VMEM(p.shape, p.dtype) for p in flat],
            pltpu.SemaphoreType.DMA((len(flat),)),
        ],
        compiler_params=params(),
        name="solve",
    )(meta, pattern, *arrays, *flat, *solved, *after)


def place_kernel(stages, *refs):
    solved, (out, joined) = refs[: len(stages)], refs[len(stages) :]
    owners, piece = solved[0].shape[0], solved[0].shape[1]
    rows = out.shape[1]
    for ref, columns in zip(solved, stages):
        for at in range(0, len(columns), 2):
            first = min(at, len(columns) - 2)
            for o in range(owners):
                start = ((o % 2) * (owners // 2) + o // 2) * piece
                joined[start : start + piece] = ref[o, :, first * rows : (first + 2) * rows]
            flipped = joined[...].T
            out[columns[first]] = flipped[:rows]
            out[columns[first + 1]] = flipped[rows:]


def place_rows(solved, stages, columns, rows):
    owners, piece, _ = solved[0].shape
    return pl.pallas_call(
        functools.partial(place_kernel, stages),
        out_shape=jax.ShapeDtypeStruct((columns, rows, owners * piece), BF16),
        in_specs=[VMEM_SPEC] * len(solved),
        out_specs=VMEM_SPEC,
        scratch_shapes=[pltpu.VMEM((owners * piece, 2 * rows), BF16)],
        compiler_params=params(),
        name="place_rows",
    )(*solved)


def staged_body(
    owners,
    known,
    outer_blocks,
    outer_row,
    outer_col,
    right_side,
    window_blocks,
    window_pattern,
    diag_inverse,
):
    own = lax.axis_index("own")
    z, x = own // 2, own % 2
    meta = jnp.stack([own, x, lax.axis_index("tile"), z, z, z ^ 1, z ^ 2, z ^ 3]).astype(jnp.int32)
    first, last = STAGES
    outer = functools.partial(
        outer_terms, meta, outer_row, outer_col, known, right_side, outer_blocks
    )
    count_0, count_1 = len(stage_blocks(first)), len(stage_blocks(last))
    own_rows = own_weights(meta, window_blocks, diag_inverse, STAGES, ())
    opposite = z_move(own_rows, 2, owners)
    send_a, keep_a = outer(CHUNKS[0][0], True, (own_rows,))
    got_a = x_move(send_a, owners)
    send_b, keep_b = outer(CHUNKS[0][1], True, (send_a,))
    got_b = x_move(send_b, owners)
    (base,) = outer(last, False, (send_b,))
    near_0 = join(own_rows, opposite, (base,), 0, count_0)
    far_0 = z_move(near_0, 1, owners)
    line_a, mine_a = pair_sum(meta, keep_a, got_a, owners, (near_0,))
    across_a = z_move(line_a, 1, owners)
    line_b, mine_b = pair_sum(meta, keep_b, got_b, owners, (line_a,))
    across_b = z_move(line_b, 1, owners)
    line_0 = join(near_0, far_0, (line_b,))
    beside_0 = x_move(line_0, owners)
    end_a, total_a = line_sum(mine_a, across_a, (line_0,))
    last_a = z_move(end_a, 2, owners)
    end_b, total_b = line_sum(mine_b, across_b, (end_a,))
    last_b = z_move(end_b, 2, owners)
    near_1 = join(own_rows, opposite, (last_b, beside_0), count_0, count_1)
    far_1 = z_move(near_1, 1, owners)
    x_near_1 = x_move(near_1, owners)
    core_line, core_beside = other_core([line_0, hold(beside_0, (end_b, last_a))])
    line = (0, 2, 1, 3)
    weights = [
        (line_0, (False, False, line)),
        (beside_0, (True, False, line)),
        (core_line, (False, True, line)),
        (core_beside, (True, True, line)),
    ]
    done = solve(
        meta,
        window_pattern,
        weights,
        first,
        (),
        (),
        CHUNKS[0],
        ((total_a, last_a), (total_b, last_b)),
        True,
        owners,
        (near_1,),
    )
    x_far_1 = x_move(hold(far_1, (x_near_1,)), owners)
    rows_0 = lax.all_to_all(done, "own", 0, 0, tiled=True)
    moved, at = [], 0
    for chunk in CHUNKS[1]:
        send, keep = cross_terms(
            meta, window_pattern, base, window_blocks, (rows_0,), chunk, at, (first,), (x_far_1,) if at else (x_near_1,)
        )
        moved.append((keep, x_move(send, owners)))
        at += len(chunk)
    parts, ends = [], []
    for index, (keep, got) in enumerate(moved):
        part, kept = pair_sum(meta, keep, got, owners, ends[: max(index - 1, 0)])
        before = [moved_end for _, moved_end in parts[: max(index - 1, 0)]]
        end, total = line_sum(kept, z_move(part, 1, owners), before)
        ends.append(end)
        parts.append((total, z_move(end, 2, owners)))
    mine = [join(near_1, far_1, moved[0][:1]), join(x_near_1, x_far_1, moved[-1][:1])]
    weights = [
        (array, (i % 2 > 0, i > 1, line)) for i, array in enumerate(mine + other_core(mine))
    ]
    solve_last = functools.partial(solve, meta, window_pattern, weights, last)
    half = solve_last((), (), CHUNKS[1][:1], parts[:1], False, owners)
    done = solve_last(CHUNKS[1][:1], (half,), CHUNKS[1][1:], parts[1:], True, owners)
    rows_1 = lax.all_to_all(done, "own", 0, 0, tiled=True)
    return place_rows([rows_0, rows_1], STAGES, right_side.shape[0], right_side.shape[1])


def plain_body(
    known,
    outer_blocks,
    outer_row,
    outer_col,
    right_side,
    window_blocks,
    window_pattern,
    diag_inverse,
):
    owner_index = lax.axis_index("own")
    columns = right_side.shape[0]
    rows_dev = right_side.shape[1]
    super_size = window_blocks.shape[3]
    sample_count = known.shape[2]
    local_row = outer_row - owner_index * known.shape[0]

    def add_block(block_index, totals):
        factor_block = lax.dynamic_index_in_dim(outer_blocks, block_index, 0, keepdims=False)
        source_row = lax.dynamic_index_in_dim(local_row, block_index, 0, keepdims=False)
        target_col = lax.dynamic_index_in_dim(outer_col, block_index, 0, keepdims=False)
        source = lax.dynamic_index_in_dim(known, source_row, 0, keepdims=False)
        product = lax.dot_general(
            factor_block, source, (((0,), (0,)), ((), ())), preferred_element_type=F32
        )
        current = lax.dynamic_index_in_dim(totals, target_col, 0, keepdims=False)
        return lax.dynamic_update_index_in_dim(totals, current + product, target_col, 0)

    outer_sum = lax.fori_loop(
        0,
        outer_blocks.shape[0],
        add_block,
        jnp.zeros((columns, super_size, sample_count), F32),
    )
    solved = jnp.zeros((columns, rows_dev, sample_count), BF16)
    for column in reversed(range(columns)):
        local_term = lax.dynamic_update_slice(
            jnp.zeros((super_size, sample_count), F32),
            right_side[column].astype(F32),
            (owner_index * rows_dev, jnp.zeros((), jnp.int32)),
        )
        pattern_mask = window_pattern[:, column].astype(BF16)
        weighted = solved * pattern_mask[:, None, None]
        window_term = jnp.einsum(
            "jrc,jrs->cs", window_blocks[:, column], weighted, preferred_element_type=F32
        )
        residual = lax.psum(local_term - outer_sum[column] - window_term, "own")
        values = lax.dot_general(
            diag_inverse[column],
            residual.astype(BF16),
            (((0,), (0,)), ((), ())),
            preferred_element_type=F32,
        )
        solved = solved.at[column].set(values.astype(BF16))
    return solved


def solution(mesh):
    owners = mesh.shape["own"]
    body = functools.partial(staged_body, owners) if owners == 8 else plain_body
    return jax.shard_map(
        body,
        mesh=mesh,
        in_specs=(
            P(("grp", "own"), None, "tile"),
            P(("grp", "own"), None, None),
            P(("grp", "own")),
            P(("grp", "own")),
            P("grp", "own", "tile"),
            P("grp", None, "own", None),
            P("grp", None),
            P("grp", None, "own"),
        ),
        out_specs=P("grp", "own", "tile"),
        check_vma=False,
    )
```
